32 devices in a mesh: grp: 2 (over y), chan: 4 (over z), seg: 2 (over x), sub: 2 (over core).
Axes of the slice: x: 2, y: 2, z: 4, core: 2. Of those that a mesh axis runs over, the one named last changes fastest.
Arguments:
- spectra: bfloat16 [8, 64, 2, 1024], P(('grp', 'seg'), 'chan', None, 'sub'), parts along dimension 0, may hold values from -6 to 6
- pair_bin: int32 [4, 4], P('chan'), may hold values from 0 to 3, as said below
Outputs:
- stacks: bfloat16 [8, 16, 16, 128], P(('grp', 'chan'), ('seg', 'sub')), parts along dimension 0
The draws below stay inside these ranges and needn't reach their ends.
There are 2 independent parts, one for each index of `grp`. The reference program is written for one: setup_inputs(seed, part) draws one part's arguments, and reference() takes and returns one part's arrays. A program takes and returns all parts, laid end to end along the dimension named above; an argument that names none is the same for every part. Nothing has to cross between parts.
Inputs may be any that keep to these rules, and one draw needn't show every extreme that they name: In each row of pair_bin one bin, the same for all rows, appears exactly 2 times and every other bin at most once; every bin appears in some row.
All inputs are finite; a program needn't handle non-finite values.
Results may differ from the reference program's by a relative error of at most 0.014.
Values may be sent and summed in bfloat16 or wider, within the bound.
A program may use at most 64 MiB of HBM per device.

```python
import math
import jax
import jax.numpy as jnp
from jax import lax

FREQ = 1024
LAGS = 128
CH_DEV = 16
SEG_DEV = 2
CH = 64
SEGS = 4
NBINS = 4
MOST = 2
N_CHAN = 4
N_SEG = 2
N_SUB = 2


def draw_pair_bin(key, part):
    order = jax.random.permutation(jax.random.fold_in(key, 11), NBINS)
    hot_bin = order[0]
    others = order[1:]
    row_ids = jnp.arange(NBINS, dtype=jnp.int32)[:, None]
    col_ids = jnp.arange(NBINS, dtype=jnp.int32)[None, :]
    other_pos = jnp.mod(row_ids + col_ids - MOST, NBINS - 1)
    bin_values = jnp.where(col_ids < MOST, hot_bin, others[other_pos])
    shuffled = jax.random.permutation(jax.random.fold_in(key, 23), bin_values, axis=1, independent=True)
    return shuffled.astype(jnp.int32)


def level_of(rng, shape, pieces, least, top_value):
    factor_of, own = 1.0, jax.random.fold_in(rng, 6)
    for position, shards_of in pieces:
        steps = jnp.exp(jax.random.uniform(jax.random.fold_in(own, position), (shards_of,), jnp.float32, least / len(pieces), top_value / len(pieces)))
        factor_of = factor_of * jnp.repeat(steps, shape[position] // shards_of).reshape([-1 if axis == position else 1 for axis in range(len(shape))])
    return factor_of


def scatter_about(own_key, extent, spread, reach, pieces=(), kind=jnp.bfloat16):
    entries = jax.random.normal(own_key, extent, jnp.float32) * spread
    if len(pieces) > 0:
        entries = level_of(own_key, extent, pieces, -0.22, 0.18) * entries
    return jnp.clip(entries, min=-reach, max=reach).astype(kind)


def setup_inputs(seed: int = 0, part: int = 0) -> dict:
    streams_of = jax.random.split(jax.random.key(seed), 3)
    own_keys = jax.random.split(jax.random.fold_in(streams_of[2], part), 3)
    return {
        "spectra": scatter_about(own_keys[0], (SEGS, CH, 2, FREQ), 0.7071, 6.0, ((0, 2), (1, 4), (3, 2))),
        "pair_bin": draw_pair_bin(jax.random.fold_in(streams_of[2], 71), part),
    }


def lag_tables():
    half_width = FREQ // N_SUB
    lag_pos = jnp.arange(LAGS, dtype=jnp.int32) - LAGS // 2
    tables = []
    for band_half in range(N_SUB):
        freq_index = band_half * half_width + jnp.arange(half_width, dtype=jnp.int32)
        phases = jnp.mod(freq_index[:, None] * lag_pos[None, :], 2 * FREQ)
        angles = phases.astype(jnp.float32) * (2.0 * math.pi / (2 * FREQ))
        weight = jnp.where(freq_index == 0, 1.0, 2.0).astype(jnp.float32)[:, None]
        tables.append(jnp.concatenate([weight * jnp.cos(angles), -weight * jnp.sin(angles)], axis=0).astype(jnp.bfloat16))
    return tables

def reference(spectra, pair_bin):
    half_width = FREQ // N_SUB
    tables = lag_tables()
    norm_scale = 1.0 / math.sqrt(SEGS * FREQ)
    blocks = spectra.reshape(SEGS, N_CHAN, CH_DEV, 2, FREQ)
    eye_mask = jnp.eye(CH_DEV, dtype=jnp.float32)
    block_ids = jnp.arange(N_CHAN, dtype=jnp.int32)
    bin_ids = jnp.arange(NBINS, dtype=jnp.int32)

    def one_row(carry, block_index):
        stacks, counts = carry
        own_block = lax.dynamic_index_in_dim(blocks, block_index, 1, keepdims=False)
        self_mask = 1.0 - (block_ids == block_index).astype(jnp.float32)[:, None, None] * eye_mask[None]
        lag_corr = jnp.zeros((N_CHAN, CH_DEV, CH_DEV, LAGS), jnp.float32)
        for seg_group in range(N_SEG):
            seg_lo = seg_group * SEG_DEV
            for band_half in range(N_SUB):
                freq_lo = band_half * half_width
                own_part = own_block[seg_lo:seg_lo + SEG_DEV, :, :, freq_lo:freq_lo + half_width].astype(jnp.float32)
                others = blocks[seg_lo:seg_lo + SEG_DEV, :, :, :, freq_lo:freq_lo + half_width].astype(jnp.float32)
                own_re = own_part[:, :, 0]
                own_im = own_part[:, :, 1]
                other_re = others[:, :, :, 0]
                other_im = others[:, :, :, 1]
                cross_re = jnp.einsum('kif,kdjf->dijf', own_re, other_re) + jnp.einsum('kif,kdjf->dijf', own_im, other_im)
                cross_im = jnp.einsum('kif,kdjf->dijf', own_im, other_re) - jnp.einsum('kif,kdjf->dijf', own_re, other_im)
                cross_spec = jnp.stack([cross_re, cross_im], axis=3) * self_mask[:, :, :, None, None]
                flat_cross = cross_spec.astype(jnp.bfloat16).reshape(N_CHAN * CH_DEV * CH_DEV, 2 * half_width)
                partial_lags = (jnp.dot(flat_cross, tables[band_half], preferred_element_type=jnp.float32) * norm_scale).astype(jnp.bfloat16)
                partial_lags = lax.optimization_barrier(partial_lags)
                lag_corr = lag_corr + partial_lags.astype(jnp.float32).reshape(N_CHAN, CH_DEV, CH_DEV, LAGS)
        bin_row = lax.dynamic_index_in_dim(pair_bin, block_index, 0, keepdims=False)
        onehot = (bin_ids[:, None] == bin_row[None, :]).astype(jnp.float32)
        stacks = stacks + jnp.einsum('qd,dijt->qijt', onehot, lag_corr, precision=lax.Precision.HIGHEST)
        counts = counts + lax.optimization_barrier(jnp.sum(onehot, axis=1))
        return ((stacks, counts), None)
    start = (jnp.zeros((NBINS, CH_DEV, CH_DEV, LAGS), jnp.float32), jnp.zeros((NBINS,), jnp.float32))
    (stacks, counts), _unused = lax.scan(one_row, start, jnp.arange(N_CHAN, dtype=jnp.int32))
    return (stacks / jnp.sqrt(counts)[:, None, None, None]).astype(jnp.bfloat16)
```

```python
import functools
import math

import jax
import jax.numpy as jnp
import numpy as np
from jax import lax
from jax.experimental import pallas as pl
from jax.experimental.pallas import tpu as pltpu
from jax.sharding import PartitionSpec as P

LAGS = 128
LANES = 128
MESH = pl.DeviceIdType.MESH


def lag_table(sub_count, half_width):
    freq_total = sub_count * half_width
    lag_pos = np.arange(LAGS) - LAGS // 2
    freq = np.arange(freq_total)
    phases = np.mod(freq[:, None] * lag_pos[None, :], 2 * freq_total)
    angles = phases.astype(np.float32) * np.float32(2.0 * math.pi / (2 * freq_total))
    weight = np.where(freq == 0, 1.0, 2.0).astype(np.float32)[:, None]
    parts = np.stack([weight * np.cos(angles), -weight * np.sin(angles)], axis=0)
    parts = parts.reshape(2, sub_count, half_width // LANES, LANES, LAGS)
    parts = parts.transpose(1, 2, 0, 3, 4).reshape(sub_count, -1, 2 * LANES, LAGS)
    return parts.astype(jnp.bfloat16)


def kernel(
    sizes, x_ref, bins_ref, table_hbm, out_ref,
    blocks, bins_all, table, wide, mixed, weights, cross, total, leave, land,
    bins_send, bins_recv, block_send, block_recv, part_send, part_recv, table_sem,
):
    chans, segs, subs, seg_dev, ch, tiles, norm = sizes
    me = lax.axis_index("chan")
    seg_me = lax.axis_index("seg")
    sub_me = lax.axis_index("sub")
    spot = seg_me * subs + sub_me
    spots = segs * subs
    out_rows = ch // spots
    unroll = chans <= 4

    load_table = pltpu.make_async_copy(table_hbm.at[sub_me], table, table_sem)
    load_table.start()

    barrier = pltpu.get_barrier_semaphore()
    for away in range(1, chans):
        pl.semaphore_signal(
            barrier, inc=1, device_id={"chan": lax.rem(me + away, chans)}, device_id_type=MESH
        )
    for away in range(1, spots):
        other = lax.rem(spot + away, spots)
        pl.semaphore_signal(
            barrier, inc=1, device_id={"seg": other // subs, "sub": lax.rem(other, subs)},
            device_id_type=MESH,
        )

    for k in range(seg_dev):
        for part in range(2):
            rows = x_ref[k, :, part, :]
            for tile in range(tiles):
                blocks[me, tile, pl.ds((k * 2 + part) * ch, ch), :] = rows[
                    :, tile * LANES : (tile + 1) * LANES
                ]
    row_ids = lax.broadcasted_iota(jnp.int32, bins_all.shape[1:], 0)
    bin_rows = jnp.full(bins_all.shape[1:], -1, jnp.int32)
    for b in range(chans):
        bin_rows = jnp.where(row_ids == b, bins_ref[0, b], bin_rows)
    bins_all[me] = bin_rows

    pl.semaphore_wait(barrier, chans - 1 + spots - 1)

    def bins_copy(source, target):
        return pltpu.make_async_remote_copy(
            src_ref=bins_all.at[source], dst_ref=bins_all.at[source],
            send_sem=bins_send.at[target], recv_sem=bins_recv.at[source],
            device_id={"chan": target}, device_id_type=MESH,
        )

    def block_copy(source, target, tile):
        return pltpu.make_async_remote_copy(
            src_ref=blocks.at[source, tile], dst_ref=blocks.at[source, tile],
            send_sem=block_send.at[target, tile], recv_sem=block_recv.at[source, tile],
            device_id={"chan": target}, device_id_type=MESH,
        )

    def part_copy(target):
        return pltpu.make_async_remote_copy(
            src_ref=leave.at[target], dst_ref=land.at[spot],
            send_sem=part_send.at[target], recv_sem=part_recv.at[spot],
            device_id={"seg": target // subs, "sub": lax.rem(target, subs)}, device_id_type=MESH,
        )

    def part_arrival(source):
        return pltpu.make_async_remote_copy(
            src_ref=leave.at[source], dst_ref=land.at[source],
            send_sem=part_send.at[source], recv_sem=part_recv.at[source],
            device_id={"seg": source // subs, "sub": lax.rem(source, subs)}, device_id_type=MESH,
        )

    others = [lax.rem(me + away, chans) for away in range(1, chans)]
    for target in others:
        bins_copy(me, target).start()
    for tile in range(tiles):
        for target in others:
            block_copy(me, target, tile).start()

    for source in others:
        bins_copy(source, source).wait_recv()
    match = (bins_all[...] == me).astype(jnp.float32)
    weights[...] = match
    pair_count = jnp.sum(jnp.sum(match, axis=0), axis=0, keepdims=True)
    scale = norm / jnp.sqrt(pair_count)

    j_ids = lax.broadcasted_iota(jnp.int32, (ch, LANES), 0)
    half = seg_dev * 2 * ch

    for tile in range(tiles):
        for source in others:
            block_copy(source, source, tile).wait_recv()

        def widen(a, carry, tile=tile):
            wide[a] = blocks[a, tile].astype(jnp.float32)
            return carry

        lax.fori_loop(0, chans, widen, 0, unroll=unroll)

        def mix(a, carry):
            diag_re, diag_im = carry

            def add(b, sums):
                weight = weights[a, pl.ds(b, 1), :]
                apart = weight * (b != a).astype(jnp.float32)
                return sums[0] + weight * wide[b], sums[1] + apart * wide[b]

            zero = jnp.zeros((half, LANES), jnp.float32)
            full, off = lax.fori_loop(0, chans, add, (zero, zero), unroll=unroll)
            mixed[a] = full
            for k in range(seg_dev):
                re, im = k * 2 * ch, (k * 2 + 1) * ch
                x_re, x_im = wide[a, pl.ds(re, ch), :], wide[a, pl.ds(im, ch), :]
                y_re, y_im = off[re : re + ch], off[im : im + ch]
                diag_re = diag_re + (x_re * y_re + x_im * y_im)
                diag_im = diag_im + (x_im * y_re - x_re * y_im)
            return diag_re, diag_im

        zero = jnp.zeros((ch, LANES), jnp.float32)
        diag_re, diag_im = lax.fori_loop(0, chans, mix, (zero, zero), unroll=unroll)

        def rows_of(group, carry):
            first = group * out_rows

            def add(a, sums):
                sums = list(sums)
                for k in range(seg_dev):
                    re, im = k * 2 * ch, (k * 2 + 1) * ch
                    y_re, y_im = mixed[a, pl.ds(re, ch), :], mixed[a, pl.ds(im, ch), :]
                    for r in range(out_rows):
                        x_re = wide[a, pl.ds(re + first + r, 1), :]
                        x_im = wide[a, pl.ds(im + first + r, 1), :]
                        sums[2 * r] = sums[2 * r] + (x_re * y_re + x_im * y_im)
                        sums[2 * r + 1] = sums[2 * r + 1] + (x_im * y_re - x_re * y_im)
                return tuple(sums)

            start = tuple(jnp.zeros((ch, LANES), jnp.float32) for _ in range(2 * out_rows))
            sums = lax.fori_loop(0, chans, add, start, unroll=unroll)
            for r in range(out_rows):
                on_diag = j_ids == first + r
                at = pl.ds(pl.multiple_of((first + r) * ch, ch), ch)
                cross[at, :LANES] = jnp.where(on_diag, diag_re, sums[2 * r]).astype(jnp.bfloat16)
                cross[at, LANES:] = jnp.where(on_diag, diag_im, sums[2 * r + 1]).astype(jnp.bfloat16)
            return carry

        lax.fori_loop(0, spots, rows_of, 0)
        if tile == 0:
            load_table.wait()
        lags = jnp.dot(cross[...], table[tile], preferred_element_type=jnp.float32)
        if tile == 0:
            total[...] = lags
        else:
            total[...] += lags

    depth = out_rows * ch
    near = [lax.rem(spot + away, spots) for away in range(1, spots)]
    for target in near:
        at = pl.ds(pl.multiple_of(target * depth, depth), depth)
        leave[target] = (total[at, :] * norm).astype(jnp.bfloat16)
        part_copy(target).start()
    own = total[pl.ds(pl.multiple_of(spot * depth, depth), depth), :] * norm
    for source in near:
        part_arrival(source).wait_recv()
        own = own + land[source].astype(jnp.float32)
    own = own * (scale / norm)
    for r in range(out_rows):
        out_ref[0, r] = own[r * ch : (r + 1) * ch].astype(jnp.bfloat16)

    for target in others:
        bins_copy(me, target).wait_send()
        for tile in range(tiles):
            block_copy(me, target, tile).wait_send()
    for target in near:
        part_copy(target).wait_send()


def local(table_all, spectra, pair_bin):
    segs, chans, subs = lax.axis_size("seg"), lax.axis_size("chan"), lax.axis_size("sub")
    seg_dev, ch, _, half_width = spectra.shape
    tiles = half_width // LANES
    spots = segs * subs
    out_rows = ch // spots
    norm = 1.0 / math.sqrt(seg_dev * segs * half_width * subs)
    rows = seg_dev * 2 * ch
    padded = -(-chans // 8) * 8
    sizes = (chans, segs, subs, seg_dev, ch, tiles, norm)
    dma = pltpu.SemaphoreType.DMA
    return pl.pallas_call(
        functools.partial(kernel, sizes),
        out_shape=jax.ShapeDtypeStruct((1, out_rows, ch, LAGS), jnp.bfloat16),
        in_specs=[
            pl.BlockSpec(memory_space=pltpu.VMEM),
            pl.BlockSpec(memory_space=pltpu.SMEM),
            pl.BlockSpec(memory_space=pl.ANY),
        ],
        out_specs=pl.BlockSpec(memory_space=pltpu.VMEM),
        scratch_shapes=[
            pltpu.VMEM((chans, tiles, rows, LANES), jnp.bfloat16),
            pltpu.VMEM((chans, padded, LANES), jnp.int32),
            pltpu.VMEM((tiles, 2 * LANES, LAGS), jnp.bfloat16),
            pltpu.VMEM((chans, rows, LANES), jnp.float32),
            pltpu.VMEM((chans, rows, LANES), jnp.float32),
            pltpu.VMEM((chans, padded, LANES), jnp.float32),
            pltpu.VMEM((ch * ch, 2 * LANES), jnp.bfloat16),
            pltpu.VMEM((ch * ch, LAGS), jnp.float32),
            pltpu.VMEM((spots, out_rows * ch, LAGS), jnp.bfloat16),
            pltpu.VMEM((spots, out_rows * ch, LAGS), jnp.bfloat16),
            dma((chans,)),
            dma((chans,)),
            dma((chans, tiles)),
            dma((chans, tiles)),
            dma((spots,)),
            dma((spots,)),
            dma,
        ],
        compiler_params=pltpu.CompilerParams(
            collective_id=0, has_side_effects=True, vmem_limit_bytes=32 * 2**20
        ),
    )(spectra, pair_bin, table_all)


def solution(mesh):
    sub_count = mesh.shape["sub"]

    def run(spectra, pair_bin):
        half_width = spectra.shape[3] // sub_count
        table_all = jnp.asarray(lag_table(sub_count, half_width))
        placed = (P(), P(("grp", "seg"), "chan", None, "sub"), P("chan", None))
        return jax.shard_map(
            local,
            mesh=mesh,
            in_specs=placed,
            out_specs=P(("grp", "chan"), ("seg", "sub"), None, None),
            check_vma=False,
        )(table_all, spectra, pair_bin)

    return run
```

```python
import functools
import math

import jax
import jax.numpy as jnp
import numpy as np
from jax import lax
from jax.experimental import pallas as pl
from jax.experimental.pallas import tpu as pltpu
from jax.sharding import PartitionSpec as P

LAGS = 128
LANES = 128
MESH = pl.DeviceIdType.MESH


def lag_table(sub_count, half_width):
    freq_total = sub_count * half_width
    lag_pos = np.arange(LAGS) - LAGS // 2
    freq = np.arange(freq_total)
    phases = np.mod(freq[:, None] * lag_pos[None, :], 2 * freq_total)
    angles = phases.astype(np.float32) * np.float32(2.0 * math.pi / (2 * freq_total))
    weight = np.where(freq == 0, 1.0, 2.0).astype(np.float32)[:, None]
    parts = np.stack([weight * np.cos(angles), -weight * np.sin(angles)], axis=0)
    parts = parts.reshape(2, sub_count, half_width // LANES, LANES, LAGS)
    parts = parts.transpose(1, 2, 0, 3, 4).reshape(sub_count, -1, 2 * LANES, LAGS)
    return parts.astype(jnp.bfloat16)


def kernel(
    sizes, x_hbm, bins_hbm, table_hbm, out_ref,
    raw, bins_all, table, wide, mixed, weights, cross, total, leave, land,
    bins_send, bins_recv, block_send, block_recv, part_send, part_recv, load_sem,
):
    chans, pair, segs, subs, seg_dev, ch, tiles, norm = sizes
    me = lax.axis_index("chan")
    spot = lax.axis_index("seg") * subs + lax.axis_index("sub")
    spots = segs * subs
    out_rows = ch // spots
    depth = out_rows * ch
    unroll = chans <= 4
    side = lax.rem(me, pair)
    base = me - side
    others = [lax.rem(me + away, chans) for away in range(1, chans)]
    near = [lax.rem(spot + away, spots) for away in range(1, spots)]

    def device(member, place):
        return {"chan": base + member, "seg": place // subs, "sub": lax.rem(place, subs)}

    barrier = pltpu.get_barrier_semaphore()
    for target in others:
        pl.semaphore_signal(barrier, inc=1, device_id={"chan": target}, device_id_type=MESH)
    for member in range(pair):
        for place in near:
            pl.semaphore_signal(
                barrier, inc=1, device_id=device(member, place), device_id_type=MESH
            )

    def lanes_of(target, tile):
        start = (lax.rem(target, pair) * tiles + tile) * LANES
        return x_hbm.at[:, :, :, pl.ds(pl.multiple_of(start, LANES), LANES)]

    own_tiles = [
        pltpu.make_async_copy(lanes_of(me, tile), raw.at[me, tile], load_sem.at[2 + tile])
        for tile in range(tiles)
    ]
    load_bins = pltpu.make_async_copy(bins_hbm, bins_all.at[me], load_sem.at[0])
    load_table = pltpu.make_async_copy(
        table_hbm.at[lax.axis_index("sub"), pl.ds(side * tiles, tiles)], table, load_sem.at[1]
    )
    load_bins.start()
    for own_tile in own_tiles:
        own_tile.start()
    load_table.start()

    pl.semaphore_wait(barrier, chans - 1 + pair * (spots - 1))

    def bins_copy(source, target):
        return pltpu.make_async_remote_copy(
            src_ref=bins_hbm, dst_ref=bins_all.at[source],
            send_sem=bins_send.at[target], recv_sem=bins_recv.at[source],
            device_id={"chan": target}, device_id_type=MESH,
        )

    def block_copy(source, target, tile):
        return pltpu.make_async_remote_copy(
            src_ref=lanes_of(target, tile), dst_ref=raw.at[source, tile],
            send_sem=block_send.at[target, tile], recv_sem=block_recv.at[source, tile],
            device_id={"chan": target}, device_id_type=MESH,
        )

    def part_copy(member, place, from_member, from_place):
        return pltpu.make_async_remote_copy(
            src_ref=leave.at[member, place], dst_ref=land.at[from_member, from_place],
            send_sem=part_send.at[member, place], recv_sem=part_recv.at[from_member, from_place],
            device_id=device(member, place), device_id_type=MESH,
        )

    for target in others:
        bins_copy(me, target).start()
    for tile in range(tiles):
        for target in others:
            block_copy(me, target, tile).start()

    load_bins.wait()
    for source in others:
        bins_copy(source, source).wait_recv()
    padded = weights.shape[2]
    row_ids = lax.broadcasted_iota(jnp.int32, (padded, chans), 0)
    col_ids = lax.broadcasted_iota(jnp.int32, (padded, chans), 1)
    wide_ids = lax.broadcasted_iota(jnp.int32, (padded, LANES), 0)

    def weigh(a, carry):
        row = jnp.broadcast_to(bins_all[a].astype(jnp.float32), (padded, chans))
        column = jnp.sum(jnp.where(row_ids == col_ids, row, 0.0), axis=1, keepdims=True)
        column = jnp.where(wide_ids < chans, jnp.broadcast_to(column, (padded, LANES)), -1.0)
        for member in range(pair):
            weights[member, a] = (column == (base + member).astype(jnp.float32)).astype(jnp.float32)
        return carry

    lax.fori_loop(0, chans, weigh, 0, unroll=unroll)
    pair_count = jnp.sum(jnp.sum(weights[side], axis=0), axis=0, keepdims=True)
    scale = 1.0 / jnp.sqrt(pair_count)

    j_ids = lax.broadcasted_iota(jnp.int32, (ch, LANES), 0)
    rows = seg_dev * 2 * ch

    for tile in range(tiles):
        own_tiles[tile].wait()
        for source in others:
            block_copy(source, me, tile).wait_recv()

        def widen(a, carry, tile=tile):
            for k in range(seg_dev):
                for part in range(2):
                    at = pl.ds((k * 2 + part) * ch, ch)
                    wide[a, at, :] = raw[a, tile, k, :, part, :].astype(jnp.float32)
            return carry

        lax.fori_loop(0, chans, widen, 0, unroll=unroll)

        for step in range(pair):
            member = lax.rem(side + 1 + step, pair)

            def mix(a, carry, member=member):
                diag_re, diag_im = carry

                def add(b, sums):
                    weight = weights[member, a, pl.ds(b, 1), :]
                    apart = weight * jnp.not_equal(b, a).astype(jnp.float32)
                    return sums[0] + weight * wide[b], sums[1] + apart * wide[b]

                zero = jnp.zeros((rows, LANES), jnp.float32)
                full, off = lax.fori_loop(0, chans, add, (zero, zero), unroll=unroll)
                mixed[a] = full
                for k in range(seg_dev):
                    re, im = k * 2 * ch, (k * 2 + 1) * ch
                    x_re, x_im = wide[a, pl.ds(re, ch), :], wide[a, pl.ds(im, ch), :]
                    y_re, y_im = off[re : re + ch], off[im : im + ch]
                    diag_re = diag_re + (x_re * y_re + x_im * y_im)
                    diag_im = diag_im + (x_im * y_re - x_re * y_im)
                return diag_re, diag_im

            zero = jnp.zeros((ch, LANES), jnp.float32)
            diag_re, diag_im = lax.fori_loop(0, chans, mix, (zero, zero), unroll=unroll)

            def rows_of(group, carry, diag_re=diag_re, diag_im=diag_im):
                first = group * out_rows

                def add(a, sums):
                    sums = list(sums)
                    for k in range(seg_dev):
                        re, im = k * 2 * ch, (k * 2 + 1) * ch
                        y_re, y_im = mixed[a, pl.ds(re, ch), :], mixed[a, pl.ds(im, ch), :]
                        for r in range(out_rows):
                            x_re = wide[a, pl.ds(re + first + r, 1), :]
                            x_im = wide[a, pl.ds(im + first + r, 1), :]
                            sums[2 * r] = sums[2 * r] + (x_re * y_re + x_im * y_im)
                            sums[2 * r + 1] = sums[2 * r + 1] + (x_im * y_re - x_re * y_im)
                    return tuple(sums)

                start = tuple(jnp.zeros((ch, LANES), jnp.float32) for _ in range(2 * out_rows))
                sums = lax.fori_loop(0, chans, add, start, unroll=unroll)
                for r in range(out_rows):
                    diag = j_ids == first + r
                    at = pl.ds(pl.multiple_of((first + r) * ch, ch), ch)
                    cross[at, :LANES] = jnp.where(diag, diag_re, sums[2 * r]).astype(jnp.bfloat16)
                    cross[at, LANES:] = jnp.where(diag, diag_im, sums[2 * r + 1]).astype(
                        jnp.bfloat16
                    )
                return carry

            lax.fori_loop(0, spots, rows_of, 0)
            if tile == 0 and step == 0:
                load_table.wait()
            lags = jnp.dot(cross[...], table[tile], preferred_element_type=jnp.float32)
            if tile > 0:
                lags = lags + total[member]
            if tile < tiles - 1:
                total[member] = lags
                continue
            lags = lags * norm
            for place in range(spots):
                leave[member, place] = lags[place * depth : (place + 1) * depth].astype(jnp.bfloat16)
            if step < pair - 1:
                part_copy(member, spot, side, spot).start()
            else:
                total[member] = lags
            for place in near:
                part_copy(member, place, side, spot).start()

    own = total[side, pl.ds(pl.multiple_of(spot * depth, depth), depth), :]
    for step in range(pair):
        member = lax.rem(side + 1 + step, pair)
        for place in near + [spot] * (step < pair - 1):
            part_copy(member, place, member, place).wait_recv()
            own = own + land[member, place].astype(jnp.float32)
    own = own * scale
    for r in range(out_rows):
        out_ref[0, r] = own[r * ch : (r + 1) * ch].astype(jnp.bfloat16)

    for target in others:
        bins_copy(me, target).wait_send()
        for tile in range(tiles):
            block_copy(me, target, tile).wait_send()
    for step in range(pair):
        member = lax.rem(side + 1 + step, pair)
        for place in near + [spot] * (step < pair - 1):
            part_copy(member, place, side, spot).wait_send()


def local(table_all, spectra, pair_bin):
    segs, chans, subs = lax.axis_size("seg"), lax.axis_size("chan"), lax.axis_size("sub")
    seg_dev, ch, _, half_width = spectra.shape
    pair = 2 if chans % 2 == 0 else 1
    tiles = half_width // LANES // pair
    spots = segs * subs
    out_rows = ch // spots
    norm = 1.0 / math.sqrt(seg_dev * segs * half_width * subs)
    rows = seg_dev * 2 * ch
    padded = -(-chans // 8) * 8
    sizes = (chans, pair, segs, subs, seg_dev, ch, tiles, norm)
    dma = pltpu.SemaphoreType.DMA
    in_hbm = pl.BlockSpec(memory_space=pl.ANY)
    return pl.pallas_call(
        functools.partial(kernel, sizes),
        out_shape=pltpu.VMEM((1, out_rows, ch, LAGS), jnp.bfloat16),
        in_specs=[in_hbm, in_hbm, in_hbm],
        out_specs=pl.BlockSpec(memory_space=pltpu.VMEM),
        scratch_shapes=[
            pltpu.VMEM((chans, tiles, seg_dev, ch, 2, LANES), jnp.bfloat16),
            pltpu.VMEM((chans, 1, chans), jnp.int32),
            pltpu.VMEM((tiles, 2 * LANES, LAGS), jnp.bfloat16),
            pltpu.VMEM((chans, rows, LANES), jnp.float32),
            pltpu.VMEM((chans, rows, LANES), jnp.float32),
            pltpu.VMEM((pair, chans, padded, LANES), jnp.float32),
            pltpu.VMEM((ch * ch, 2 * LANES), jnp.bfloat16),
            pltpu.VMEM((pair, ch * ch, LAGS), jnp.float32),
            pltpu.VMEM((pair, spots, out_rows * ch, LAGS), jnp.bfloat16),
            pltpu.VMEM((pair, spots, out_rows * ch, LAGS), jnp.bfloat16),
            dma((chans,)),
            dma((chans,)),
            dma((chans, tiles)),
            dma((chans, tiles)),
            dma((pair, spots)),
            dma((pair, spots)),
            dma((2 + tiles,)),
        ],
        compiler_params=pltpu.CompilerParams(
            collective_id=0, has_side_effects=True, vmem_limit_bytes=60 * 2**20
        ),
    )(spectra, pair_bin, table_all)


def solution(mesh):
    sub_count = mesh.shape["sub"]

    def run(spectra, pair_bin):
        half_width = spectra.shape[3] // sub_count
        table_all = jnp.asarray(lag_table(sub_count, half_width))
        placed = (P(), P(("grp", "seg"), "chan", None, "sub"), P("chan", None))
        return jax.shard_map(
            local,
            mesh=mesh,
            in_specs=placed,
            out_specs=P(("grp", "chan"), ("seg", "sub"), None, None),
            check_vma=False,
        )(table_all, spectra, pair_bin)

    return run
```

```python
import functools
import math

import jax
import jax.numpy as jnp
import numpy as np
from jax import lax
from jax.experimental import pallas as pl
from jax.experimental.pallas import tpu as pltpu
from jax.sharding import PartitionSpec as P

LAGS = 128
LANES = 128
MESH = pl.DeviceIdType.MESH


def lag_table(sub_count, half_width):
    freq_total = sub_count * half_width
    lag_pos = np.arange(LAGS) - LAGS // 2
    freq = np.arange(freq_total)
    phases = np.mod(freq[:, None] * lag_pos[None, :], 2 * freq_total)
    angles = phases.astype(np.float32) * np.float32(2.0 * math.pi / (2 * freq_total))
    weight = np.where(freq == 0, 1.0, 2.0).astype(np.float32)[:, None]
    parts = np.stack([weight * np.cos(angles), -weight * np.sin(angles)], axis=0)
    parts = parts.reshape(2, sub_count, half_width // LANES, LANES, LAGS)
    parts = parts.transpose(1, 2, 0, 3, 4).reshape(sub_count, -1, 2 * LANES, LAGS)
    return parts.astype(jnp.bfloat16)


def kernel(
    sizes, x_hbm, bins_hbm, table_hbm, out_ref,
    own, raw, bins_all, table, wide, mixed, weights, total, leave, land,
    bins_send, bins_recv, block_send, block_recv, part_send, part_recv, load_sem,
):
    chans, pair, segs, subs, seg_dev, ch, tiles, norm = sizes
    me = lax.axis_index("chan")
    spot = lax.axis_index("seg") * subs + lax.axis_index("sub")
    spots = segs * subs
    out_rows = ch // spots
    unroll = chans <= 4
    side = lax.rem(me, pair)
    base = me - side
    others = [lax.rem(me + away, chans) for away in range(1, chans)]
    aways = list(range(subs, spots)) + list(range(1, subs))
    near = [
        lax.rem(spot // subs + away // subs, segs) * subs + lax.rem(spot + away, subs)
        for away in aways
    ]

    def device(member, place):
        return {"chan": base + member, "seg": place // subs, "sub": lax.rem(place, subs)}

    barrier = pltpu.get_barrier_semaphore()
    for target in others:
        pl.semaphore_signal(barrier, inc=1, device_id={"chan": target}, device_id_type=MESH)
    for member in range(pair):
        for place in near:
            pl.semaphore_signal(
                barrier, inc=1, device_id=device(member, place), device_id_type=MESH
            )

    loads = [
        pltpu.make_async_copy(
            x_hbm.at[:, :, :, lane * LANES : (lane + 1) * LANES], own.at[lane], load_sem.at[2 + lane]
        )
        for lane in range(pair * tiles)
    ]
    load_bins = pltpu.make_async_copy(bins_hbm, bins_all.at[me], load_sem.at[0])
    load_table = pltpu.make_async_copy(
        table_hbm.at[lax.axis_index("sub"), pl.ds(side * tiles, tiles)], table, load_sem.at[1]
    )
    load_bins.start()
    for load in loads:
        load.start()
    load_table.start()

    load_bins.wait()
    for load in loads:
        load.wait()
    pl.semaphore_wait(barrier, chans - 1 + pair * (spots - 1))

    def bins_copy(source, target):
        return pltpu.make_async_remote_copy(
            src_ref=bins_all.at[me], dst_ref=bins_all.at[source],
            send_sem=bins_send.at[target], recv_sem=bins_recv.at[source],
            device_id={"chan": target}, device_id_type=MESH,
        )

    def block_copy(source, target, tile):
        return pltpu.make_async_remote_copy(
            src_ref=own.at[lax.rem(target, pair) * tiles + tile], dst_ref=raw.at[source, tile],
            send_sem=block_send.at[target, tile], recv_sem=block_recv.at[source, tile],
            device_id={"chan": target}, device_id_type=MESH,
        )

    def part_copy(member, place, from_member, from_place):
        return pltpu.make_async_remote_copy(
            src_ref=leave.at[member, place], dst_ref=land.at[from_member, from_place],
            send_sem=part_send.at[member, place], recv_sem=part_recv.at[from_member, from_place],
            device_id=device(member, place), device_id_type=MESH,
        )

    for target in others:
        bins_copy(me, target).start()
    for tile in range(tiles):
        for target in others:
            block_copy(me, target, tile).start()

    for tile in range(tiles):
        raw[me, tile] = own[side * tiles + tile]
    for source in others:
        bins_copy(source, source).wait_recv()
    padded = weights.shape[2]
    row_ids = lax.broadcasted_iota(jnp.int32, (padded, chans), 0)
    col_ids = lax.broadcasted_iota(jnp.int32, (padded, chans), 1)
    wide_ids = lax.broadcasted_iota(jnp.int32, (padded, LANES), 0)

    def weigh(a, carry):
        row = jnp.broadcast_to(bins_all[a].astype(jnp.float32), (padded, chans))
        column = jnp.sum(jnp.where(row_ids == col_ids, row, 0.0), axis=1, keepdims=True)
        column = jnp.where(wide_ids < chans, jnp.broadcast_to(column, (padded, LANES)), -1.0)
        for member in range(pair):
            weights[member, a] = (column == (base + member).astype(jnp.float32)).astype(jnp.float32)
        return carry

    lax.fori_loop(0, chans, weigh, 0, unroll=unroll)
    pair_count = jnp.sum(jnp.sum(weights[side], axis=0), axis=0, keepdims=True)
    scale = 1.0 / jnp.sqrt(pair_count)

    j_ids = lax.broadcasted_iota(jnp.int32, (ch, LANES), 0)
    rows = seg_dev * 2 * ch

    for tile in range(tiles):
        for source in others:
            block_copy(source, me, tile).wait_recv()

        def widen(a, carry, tile=tile):
            for k in range(seg_dev):
                for part in range(2):
                    at = pl.ds((k * 2 + part) * ch, ch)
                    wide[a, at, :] = raw[a, tile, k, :, part, :].astype(jnp.float32)
            return carry

        lax.fori_loop(0, chans, widen, 0, unroll=unroll)

        for step in range(pair):
            member = lax.rem(side + 1 + step, pair)

            def mix(a, carry, member=member):
                diag_re, diag_im = carry

                def add(b, sums):
                    weight = weights[member, a, pl.ds(b, 1), :]
                    apart = weight * jnp.not_equal(b, a).astype(jnp.float32)
                    return sums[0] + weight * wide[b], sums[1] + apart * wide[b]

                zero = jnp.zeros((rows, LANES), jnp.float32)
                full, off = lax.fori_loop(0, chans, add, (zero, zero), unroll=unroll)
                mixed[a] = full
                for k in range(seg_dev):
                    re, im = k * 2 * ch, (k * 2 + 1) * ch
                    x_re, x_im = wide[a, pl.ds(re, ch), :], wide[a, pl.ds(im, ch), :]
                    y_re, y_im = off[re : re + ch], off[im : im + ch]
                    diag_re = diag_re + (x_re * y_re + x_im * y_im)
                    diag_im = diag_im + (x_im * y_re - x_re * y_im)
                return diag_re, diag_im

            zero = jnp.zeros((ch, LANES), jnp.float32)
            diag_re, diag_im = lax.fori_loop(0, chans, mix, (zero, zero), unroll=unroll)

            last = tile == tiles - 1
            if tile == 0 and step == 0:
                load_table.wait()
            for place in near + [spot]:
                first = place * out_rows

                def add(a, sums, first=first):
                    sums = list(sums)
                    for k in range(seg_dev):
                        re, im = k * 2 * ch, (k * 2 + 1) * ch
                        y_re, y_im = mixed[a, pl.ds(re, ch), :], mixed[a, pl.ds(im, ch), :]
                        for r in range(out_rows):
                            x_re = wide[a, pl.ds(re + first + r, 1), :]
                            x_im = wide[a, pl.ds(im + first + r, 1), :]
                            sums[2 * r] = sums[2 * r] + (x_re * y_re + x_im * y_im)
                            sums[2 * r + 1] = sums[2 * r + 1] + (x_im * y_re - x_re * y_im)
                    return tuple(sums)

                start = tuple(jnp.zeros((ch, LANES), jnp.float32) for _ in range(2 * out_rows))
                sums = lax.fori_loop(0, chans, add, start, unroll=unroll)
                pieces = []
                for r in range(out_rows):
                    diag = j_ids == first + r
                    pieces.append(
                        jnp.concatenate(
                            [
                                jnp.where(diag, diag_re, sums[2 * r]).astype(jnp.bfloat16),
                                jnp.where(diag, diag_im, sums[2 * r + 1]).astype(jnp.bfloat16),
                            ],
                            axis=1,
                        )
                    )
                cross = jnp.concatenate(pieces, axis=0)
                lags = jnp.dot(cross, table[tile], preferred_element_type=jnp.float32)
                if tile > 0:
                    lags = lags + total[member, place]
                if not last:
                    total[member, place] = lags
                    continue
                lags = lags * norm
                if step == pair - 1 and place is spot:
                    total[side, spot] = lags
                else:
                    leave[member, place] = lags.astype(jnp.bfloat16)
                    part_copy(member, place, side, spot).start()

    result = total[side, spot]
    for step in range(pair):
        member = lax.rem(side + 1 + step, pair)
        for place in near + [spot] * (step < pair - 1):
            part_copy(member, place, member, place).wait_recv()
            result = result + land[member, place].astype(jnp.float32)
    result = result * scale
    for r in range(out_rows):
        out_ref[0, r] = result[r * ch : (r + 1) * ch].astype(jnp.bfloat16)

    for target in others:
        bins_copy(me, target).wait_send()
        for tile in range(tiles):
            block_copy(me, target, tile).wait_send()
    for step in range(pair):
        member = lax.rem(side + 1 + step, pair)
        for place in near + [spot] * (step < pair - 1):
            part_copy(member, place, side, spot).wait_send()


def local(table_all, spectra, pair_bin):
    segs, chans, subs = lax.axis_size("seg"), lax.axis_size("chan"), lax.axis_size("sub")
    seg_dev, ch, _, half_width = spectra.shape
    pair = 2 if chans % 2 == 0 else 1
    tiles = half_width // LANES // pair
    spots = segs * subs
    out_rows = ch // spots
    norm = 1.0 / math.sqrt(seg_dev * segs * half_width * subs)
    rows = seg_dev * 2 * ch
    padded = -(-chans // 8) * 8
    sizes = (chans, pair, segs, subs, seg_dev, ch, tiles, norm)
    dma = pltpu.SemaphoreType.DMA
    in_hbm = pl.BlockSpec(memory_space=pl.ANY)
    return pl.pallas_call(
        functools.partial(kernel, sizes),
        out_shape=pltpu.VMEM((1, out_rows, ch, LAGS), jnp.bfloat16),
        in_specs=[in_hbm, in_hbm, in_hbm],
        out_specs=pl.BlockSpec(memory_space=pltpu.VMEM),
        scratch_shapes=[
            pltpu.VMEM((pair * tiles, seg_dev, ch, 2, LANES), jnp.bfloat16),
            pltpu.VMEM((chans, tiles, seg_dev, ch, 2, LANES), jnp.bfloat16),
            pltpu.VMEM((chans, 1, chans), jnp.int32),
            pltpu.VMEM((tiles, 2 * LANES, LAGS), jnp.bfloat16),
            pltpu.VMEM((chans, rows, LANES), jnp.float32),
            pltpu.VMEM((chans, rows, LANES), jnp.float32),
            pltpu.VMEM((pair, chans, padded, LANES), jnp.float32),
            pltpu.VMEM((pair, spots, out_rows * ch, LAGS), jnp.float32),
            pltpu.VMEM((pair, spots, out_rows * ch, LAGS), jnp.bfloat16),
            pltpu.VMEM((pair, spots, out_rows * ch, LAGS), jnp.bfloat16),
            dma((chans,)),
            dma((chans,)),
            dma((chans, tiles)),
            dma((chans, tiles)),
            dma((pair, spots)),
            dma((pair, spots)),
            dma((2 + pair * tiles,)),
        ],
        compiler_params=pltpu.CompilerParams(
            collective_id=0, has_side_effects=True, vmem_limit_bytes=60 * 2**20
        ),
    )(spectra, pair_bin, table_all)


def solution(mesh):
    sub_count = mesh.shape["sub"]

    def run(spectra, pair_bin):
        half_width = spectra.shape[3] // sub_count
        table_all = jnp.asarray(lag_table(sub_count, half_width))
        placed = (P(), P(("grp", "seg"), "chan", None, "sub"), P("chan", None))
        return jax.shard_map(
            local,
            mesh=mesh,
            in_specs=placed,
            out_specs=P(("grp", "chan"), ("seg", "sub"), None, None),
            check_vma=False,
        )(table_all, spectra, pair_bin)

    return run
```

```python
import functools
import math

import jax
import jax.numpy as jnp
import numpy as np
from jax import lax
from jax.experimental import pallas as pl
from jax.experimental.pallas import tpu as pltpu
from jax.sharding import PartitionSpec as P

LAGS = 128
LANES = 128
MESH = pl.DeviceIdType.MESH


def lag_table(sub_count, half_width):
    freq_total = sub_count * half_width
    lag_pos = np.arange(LAGS) - LAGS // 2
    freq = np.arange(freq_total)
    phases = np.mod(freq[:, None] * lag_pos[None, :], 2 * freq_total)
    angles = phases.astype(np.float32) * np.float32(2.0 * math.pi / (2 * freq_total))
    weight = np.where(freq == 0, 1.0, 2.0).astype(np.float32)[:, None]
    parts = np.stack([weight * np.cos(angles), -weight * np.sin(angles)], axis=0)
    parts = parts.reshape(2, sub_count, half_width // LANES, LANES, LAGS)
    parts = parts.transpose(1, 2, 0, 3, 4).reshape(sub_count, -1, 2 * LANES, LAGS)
    return parts.astype(jnp.bfloat16)


def kernel(
    sizes, x_hbm, bins_hbm, table_hbm, out_ref,
    own, raw, bins_all, table, wide, mixed, weights, total, leave, land,
    bins_send, bins_recv, block_send, block_recv, part_send, part_recv, load_sem,
):
    chans, pair, segs, subs, seg_dev, ch, tiles, norm = sizes
    me = lax.axis_index("chan")
    spot = lax.axis_index("seg") * subs + lax.axis_index("sub")
    spots = segs * subs
    out_rows = ch // spots
    unroll = chans <= 4
    side = lax.rem(me, pair)
    base = me - side
    others = [lax.rem(me + away, chans) for away in range(1, chans)]
    aways = list(range(subs, spots)) + list(range(1, subs))
    near = [
        lax.rem(spot // subs + away // subs, segs) * subs + lax.rem(spot + away, subs)
        for away in aways
    ]

    def device(member, place):
        return {"chan": base + member, "seg": place // subs, "sub": lax.rem(place, subs)}

    barrier = pltpu.get_barrier_semaphore()
    for target in others:
        pl.semaphore_signal(barrier, inc=1, device_id={"chan": target}, device_id_type=MESH)
    for member in range(pair):
        for place in near:
            pl.semaphore_signal(
                barrier, inc=1, device_id=device(member, place), device_id_type=MESH
            )

    loads = [
        pltpu.make_async_copy(
            x_hbm.at[:, :, :, lane * LANES : (lane + 1) * LANES], own.at[lane], load_sem.at[2 + lane]
        )
        for lane in range(pair * tiles)
    ]
    load_bins = pltpu.make_async_copy(bins_hbm, bins_all.at[me], load_sem.at[0])
    load_table = pltpu.make_async_copy(
        table_hbm.at[lax.axis_index("sub"), pl.ds(side * tiles, tiles)], table, load_sem.at[1]
    )
    load_bins.start()
    for load in loads:
        load.start()
    load_table.start()

    load_bins.wait()
    for load in loads:
        load.wait()
    pl.semaphore_wait(barrier, chans - 1 + pair * (spots - 1))

    def bins_copy(source, target):
        return pltpu.make_async_remote_copy(
            src_ref=bins_all.at[me], dst_ref=bins_all.at[source],
            send_sem=bins_send.at[target], recv_sem=bins_recv.at[source],
            device_id={"chan": target}, device_id_type=MESH,
        )

    def block_copy(source, target, tile):
        return pltpu.make_async_remote_copy(
            src_ref=own.at[lax.rem(target, pair) * tiles + tile], dst_ref=raw.at[source, tile],
            send_sem=block_send.at[target, tile], recv_sem=block_recv.at[source, tile],
            device_id={"chan": target}, device_id_type=MESH,
        )

    def part_copy(member, place, from_member, from_place):
        return pltpu.make_async_remote_copy(
            src_ref=leave.at[member, place], dst_ref=land.at[from_member, from_place],
            send_sem=part_send.at[member, place], recv_sem=part_recv.at[from_member, from_place],
            device_id=device(member, place), device_id_type=MESH,
        )

    for target in others:
        bins_copy(me, target).start()
    for tile in range(tiles):
        for target in others:
            block_copy(me, target, tile).start()

    for tile in range(tiles):
        raw[me, tile] = own[side * tiles + tile]
    for source in others:
        bins_copy(source, source).wait_recv()
    padded = weights.shape[2]
    row_ids = lax.broadcasted_iota(jnp.int32, (padded, chans), 0)
    col_ids = lax.broadcasted_iota(jnp.int32, (padded, chans), 1)
    wide_ids = lax.broadcasted_iota(jnp.int32, (padded, LANES), 0)

    def weigh(a, carry):
        row = jnp.broadcast_to(bins_all[a].astype(jnp.float32), (padded, chans))
        column = jnp.sum(jnp.where(row_ids == col_ids, row, 0.0), axis=1, keepdims=True)
        column = jnp.where(wide_ids < chans, jnp.broadcast_to(column, (padded, LANES)), -1.0)
        for member in range(pair):
            weights[member, a] = (column == (base + member).astype(jnp.float32)).astype(jnp.float32)
        return carry

    lax.fori_loop(0, chans, weigh, 0, unroll=unroll)
    pair_count = jnp.sum(jnp.sum(weights[side], axis=0), axis=0, keepdims=True)
    scale = 1.0 / jnp.sqrt(pair_count)

    j_ids = lax.broadcasted_iota(jnp.int32, (ch, LANES), 0)
    rows = seg_dev * 2 * ch

    for tile in range(tiles):
        for source in others:
            block_copy(source, me, tile).wait_recv()

        def widen(a, carry, tile=tile):
            for k in range(seg_dev):
                for part in range(2):
                    at = pl.ds((k * 2 + part) * ch, ch)
                    wide[a, at, :] = raw[a, tile, k, :, part, :].astype(jnp.float32)
            return carry

        lax.fori_loop(0, chans, widen, 0, unroll=unroll)

        for step in range(pair):
            member = lax.rem(side + 1 + step, pair)

            def mix(a, carry, member=member):
                diag_re, diag_im = carry

                def add(b, sums):
                    weight = weights[member, a, pl.ds(b, 1), :]
                    apart = weight * jnp.not_equal(b, a).astype(jnp.float32)
                    return sums[0] + weight * wide[b], sums[1] + apart * wide[b]

                zero = jnp.zeros((rows, LANES), jnp.float32)
                full, off = lax.fori_loop(0, chans, add, (zero, zero), unroll=unroll)
                mixed[a] = full
                for k in range(seg_dev):
                    re, im = k * 2 * ch, (k * 2 + 1) * ch
                    x_re, x_im = wide[a, pl.ds(re, ch), :], wide[a, pl.ds(im, ch), :]
                    y_re, y_im = off[re : re + ch], off[im : im + ch]
                    diag_re = diag_re + (x_re * y_re + x_im * y_im)
                    diag_im = diag_im + (x_im * y_re - x_re * y_im)
                return diag_re, diag_im

            zero = jnp.zeros((ch, LANES), jnp.float32)
            diag_re, diag_im = lax.fori_loop(0, chans, mix, (zero, zero), unroll=unroll)

            last = tile == tiles - 1
            if tile == 0 and step == 0:
                load_table.wait()
            crosses = []
            for turn, place in enumerate(near + [spot]):
                first = place * out_rows

                def add(a, sums, first=first):
                    sums = list(sums)
                    for k in range(seg_dev):
                        re, im = k * 2 * ch, (k * 2 + 1) * ch
                        y_re, y_im = mixed[a, pl.ds(re, ch), :], mixed[a, pl.ds(im, ch), :]
                        for r in range(out_rows):
                            x_re = wide[a, pl.ds(re + first + r, 1), :]
                            x_im = wide[a, pl.ds(im + first + r, 1), :]
                            sums[2 * r] = sums[2 * r] + (x_re * y_re + x_im * y_im)
                            sums[2 * r + 1] = sums[2 * r + 1] + (x_im * y_re - x_re * y_im)
                    return tuple(sums)

                start = tuple(jnp.zeros((ch, LANES), jnp.float32) for _ in range(2 * out_rows))
                sums = lax.fori_loop(0, chans, add, start, unroll=unroll)
                pieces = []
                for r in range(out_rows):
                    diag = j_ids == first + r
                    pieces.append(
                        jnp.concatenate(
                            [
                                jnp.where(diag, diag_re, sums[2 * r]).astype(jnp.bfloat16),
                                jnp.where(diag, diag_im, sums[2 * r + 1]).astype(jnp.bfloat16),
                            ],
                            axis=1,
                        )
                    )
                cross = jnp.concatenate(pieces, axis=0)
                if not last:
                    crosses.append(cross)
                    continue
                lags = jnp.dot(cross, table[tile], preferred_element_type=jnp.float32)
                if tile > 0:
                    lags = lags + total[step, turn]
                lags = lags * norm
                if step == pair - 1 and place is spot:
                    result = lags
                else:
                    leave[member, place] = lags.astype(jnp.bfloat16)
                    part_copy(member, place, side, spot).start()
            if not last:
                lags = jnp.dot(
                    jnp.concatenate(crosses, axis=0), table[tile], preferred_element_type=jnp.float32
                ).reshape(total.shape[1:])
                total[step] = lags if tile == 0 else lags + total[step]

    for step in range(pair):
        member = lax.rem(side + 1 + step, pair)
        for place in near + [spot] * (step < pair - 1):
            part_copy(member, place, member, place).wait_recv()
            result = result + land[member, place].astype(jnp.float32)
    result = result * scale
    for r in range(out_rows):
        out_ref[0, r] = result[r * ch : (r + 1) * ch].astype(jnp.bfloat16)

    for target in others:
        bins_copy(me, target).wait_send()
        for tile in range(tiles):
            block_copy(me, target, tile).wait_send()
    for step in range(pair):
        member = lax.rem(side + 1 + step, pair)
        for place in near + [spot] * (step < pair - 1):
            part_copy(member, place, side, spot).wait_send()


def local(table_all, spectra, pair_bin):
    segs, chans, subs = lax.axis_size("seg"), lax.axis_size("chan"), lax.axis_size("sub")
    seg_dev, ch, _, half_width = spectra.shape
    pair = 2 if chans % 2 == 0 else 1
    tiles = half_width // LANES // pair
    spots = segs * subs
    out_rows = ch // spots
    norm = 1.0 / math.sqrt(seg_dev * segs * half_width * subs)
    rows = seg_dev * 2 * ch
    padded = -(-chans // 8) * 8
    sizes = (chans, pair, segs, subs, seg_dev, ch, tiles, norm)
    dma = pltpu.SemaphoreType.DMA
    in_hbm = pl.BlockSpec(memory_space=pl.ANY)
    return pl.pallas_call(
        functools.partial(kernel, sizes),
        out_shape=pltpu.VMEM((1, out_rows, ch, LAGS), jnp.bfloat16),
        in_specs=[in_hbm, in_hbm, in_hbm],
        out_specs=pl.BlockSpec(memory_space=pltpu.VMEM),
        scratch_shapes=[
            pltpu.VMEM((pair * tiles, seg_dev, ch, 2, LANES), jnp.bfloat16),
            pltpu.VMEM((chans, tiles, seg_dev, ch, 2, LANES), jnp.bfloat16),
            pltpu.VMEM((chans, 1, chans), jnp.int32),
            pltpu.VMEM((tiles, 2 * LANES, LAGS), jnp.bfloat16),
            pltpu.VMEM((chans, rows, LANES), jnp.float32),
            pltpu.VMEM((chans, rows, LANES), jnp.float32),
            pltpu.VMEM((pair, chans, padded, LANES), jnp.float32),
            pltpu.VMEM((pair, spots, out_rows * ch, LAGS), jnp.float32),
            pltpu.VMEM((pair, spots, out_rows * ch, LAGS), jnp.bfloat16),
            pltpu.VMEM((pair, spots, out_rows * ch, LAGS), jnp.bfloat16),
            dma((chans,)),
            dma((chans,)),
            dma((chans, tiles)),
            dma((chans, tiles)),
            dma((pair, spots)),
            dma((pair, spots)),
            dma((2 + pair * tiles,)),
        ],
        compiler_params=pltpu.CompilerParams(
            collective_id=0, has_side_effects=True, vmem_limit_bytes=60 * 2**20
        ),
    )(spectra, pair_bin, table_all)


def solution(mesh):
    sub_count = mesh.shape["sub"]

    def run(spectra, pair_bin):
        half_width = spectra.shape[3] // sub_count
        table_all = jnp.asarray(lag_table(sub_count, half_width))
        placed = (P(), P(("grp", "seg"), "chan", None, "sub"), P("chan", None))
        return jax.shard_map(
            local,
            mesh=mesh,
            in_specs=placed,
            out_specs=P(("grp", "chan"), ("seg", "sub"), None, None),
            check_vma=False,
        )(table_all, spectra, pair_bin)

    return run
```
